256 devices in a mesh: ctx: 64 (over y, x, z_lo), head: 4 (over z_hi, core).
Axes of the slice: x: 4, y: 4, z: 8 (z_hi: 2, z_lo: 4; z = z_hi * 4 + z_lo), core: 2. Of those that a mesh axis runs over, the one named last changes fastest.
Arguments:
- queries: bfloat16 [32768, 16, 128], P('ctx', 'head'), may hold values from -6 to 6, as said below
- keys: bfloat16 [32768, 4, 128], P('ctx', 'head'), may hold values from -6 to 6, as said below
- values: bfloat16 [32768, 4, 128], P('ctx', 'head'), may hold values from -6 to 6
- w_out: bfloat16 [2048, 4096], P('head'), may hold values from -0.125 to 0.125
- block_order: int32 [64], replicated, may hold values from 0 to 63, as said below
- chosen: int32 [64, 4, 3], P('ctx', 'head'), may hold values from 0 to 62, as said below
Outputs:
- projected: bfloat16 [32768, 4096], P('ctx', 'head')
The draws below stay inside these ranges and needn't reach their ends.
Inputs may be any that keep to these rules, and one draw needn't show every extreme that they name: `block_order`: A permutation of the sequence blocks; tokens keep their sequence order inside a stored block. For stored block s with sequence block b = block_order[s]: the entries of chosen[s, k] are distinct and below b, except that when b < 3 the last 3 - b entries equal b and choose nothing. `queries`: bounded entries. `keys`: bounded entries.
All inputs are finite; a program needn't handle non-finite values.
Results may differ from the reference program's by a relative error of at most 0.0056.
Values may be sent and summed in bfloat16 or wider, within the bound.
No kernel may reach another device: no remote copies, remote signals or barrier semaphores. Data moves between devices by JAX's collectives and lax.ppermute only.
A program may use at most 128 MiB of HBM per device.

```python
import jax
import jax.numpy as jnp
from jax import lax

D = 4096
QUERY_HEADS = 16
KEY_VALUE_HEADS = 4
HEAD_SIZE = 128
BLK = 512
TOPK = 3
TOKEN_COUNT = 32768
BLOCK_COUNT = 64


def shared_order(key):
    return jax.random.permutation(jax.random.fold_in(key, 99), BLOCK_COUNT).astype(jnp.int32)


def draw_queries(key, part):
    key = jax.random.fold_in(key, 1)
    sampled_values = jax.random.truncated_normal(key, -6.0, 6.0, (TOKEN_COUNT, QUERY_HEADS, HEAD_SIZE), jnp.float32)
    return sampled_values.astype(jnp.bfloat16)


def draw_keys(key, part):
    key = jax.random.fold_in(key, 2)
    sampled_values = jax.random.truncated_normal(key, -6.0, 6.0, (TOKEN_COUNT, KEY_VALUE_HEADS, HEAD_SIZE), jnp.float32)
    return sampled_values.astype(jnp.bfloat16)


def draw_block_order(key, part):
    return shared_order(key)


def draw_chosen(key, part):
    stored_order = shared_order(key)
    key = jax.random.fold_in(key, 3)
    candidates = jnp.arange(BLOCK_COUNT, dtype=jnp.int32)
    small_noise = jax.random.randint(key, (BLOCK_COUNT, KEY_VALUE_HEADS, BLOCK_COUNT), 0, 4096, dtype=jnp.int32)
    favour = jnp.where(candidates < 2, 3000, 0).astype(jnp.int32)
    neighbour = jnp.where(candidates[None, None, :] == stored_order[:, None, None] - 1, 10000, 0).astype(jnp.int32)
    usable = candidates[None, None, :] < stored_order[:, None, None]
    ranked = jnp.where(usable, (small_noise + favour[None, None, :] + neighbour) * (2 * BLOCK_COUNT) + candidates[None, None, :], -1 - candidates[None, None, :])
    picked = lax.top_k(ranked, TOPK)[1].astype(jnp.int32)
    filled = jnp.arange(TOPK, dtype=jnp.int32)[None, None, :] < stored_order[:, None, None]
    return jnp.where(filled, picked, stored_order[:, None, None]).astype(jnp.int32)


def levels(stream_key, extent, shards, least, largest):
    loudness, own = 1.0, jax.random.fold_in(stream_key, 6)
    for dim, blocks in shards:
        heights = jnp.exp(jax.random.uniform(jax.random.fold_in(own, dim), (blocks,), jnp.float32, least / len(shards), largest / len(shards)))
        loudness = loudness * jnp.repeat(heights, extent[dim] // blocks).reshape([-1 if axis == dim else 1 for axis in range(len(extent))])
    return loudness


def centred(rng, extent, scale, most, cuts=(), kind=jnp.bfloat16):
    result = scale * jax.random.normal(rng, extent, jnp.float32)
    if cuts:
        result = result * levels(rng, extent, cuts, -0.22, 0.18)
    return jnp.clip(result, -most, most).astype(kind)


def setup_inputs(seed: int = 0) -> dict:
    arg_keys = jax.random.split(jax.random.key(seed), 7)
    queries = draw_queries(jax.random.fold_in(arg_keys[6], 71), 0)
    keys = draw_keys(jax.random.fold_in(arg_keys[6], 71), 0)
    values = centred(arg_keys[2], (TOKEN_COUNT, KEY_VALUE_HEADS, HEAD_SIZE), 1.0, 6.0, ((0, 64), (1, 4)))
    w_out = centred(arg_keys[3], (QUERY_HEADS * HEAD_SIZE, D), (QUERY_HEADS * HEAD_SIZE) ** -0.5, 0.125, ((0, 4),))
    block_order = draw_block_order(jax.random.fold_in(arg_keys[6], 71), 0)
    chosen = draw_chosen(jax.random.fold_in(arg_keys[6], 71), 0)
    return dict(queries=queries, keys=keys, values=values, w_out=w_out, block_order=block_order, chosen=chosen)


def attend_block(query_blk, keys_sel, values_sel, slot_ok, keys_own, values_own):
    n_rows, kv_heads, per_group, head_dim = query_blk.shape
    factor = head_dim ** -0.5
    query_f = query_blk.astype(jnp.float32)
    far_scores = jnp.einsum("tkgd,kjsd->tkgjs", query_f, keys_sel.astype(jnp.float32)) * factor
    far_scores = far_scores.reshape(n_rows, kv_heads, per_group, -1)
    near_scores = jnp.einsum("tkgd,skd->tkgs", query_f, keys_own.astype(jnp.float32)) * factor
    scores = jnp.concatenate([far_scores, near_scores], axis=3)
    far_ok = jnp.repeat(slot_ok, n_rows, axis=1)
    far_ok = jnp.broadcast_to(far_ok[None, :, None, :], far_scores.shape)
    causal = jnp.arange(n_rows)[None, :] <= jnp.arange(n_rows)[:, None]
    near_ok = jnp.broadcast_to(causal[:, None, None, :], near_scores.shape)
    allowed = jnp.concatenate([far_ok, near_ok], axis=3)
    highest = jnp.max(jnp.where(allowed, scores, -jnp.inf), axis=3, keepdims=True)
    weights = jnp.where(allowed, jnp.exp(scores - highest), 0.0)
    totals = jnp.sum(weights, axis=3, keepdims=True)
    rounded = lax.optimization_barrier(weights.astype(jnp.bfloat16))
    all_values = jnp.concatenate([values_sel.reshape(kv_heads, -1, head_dim), jnp.transpose(values_own, (1, 0, 2))], axis=1)
    blended = jnp.einsum("tkgs,ksd->tkgd", rounded.astype(jnp.float32), all_values.astype(jnp.float32))
    return (blended / totals).astype(jnp.bfloat16).reshape(n_rows, -1)


def reference(queries, keys, values, w_out, block_order, chosen):
    q_heads = queries.shape[1]
    kv_heads = keys.shape[1]
    head_dim = keys.shape[2]
    per_group = q_heads // kv_heads
    slot_of = jnp.zeros((BLOCK_COUNT,), jnp.int32).at[block_order].set(jnp.arange(BLOCK_COUNT, dtype=jnp.int32))
    chosen_slots = slot_of[chosen]
    slot_ok = chosen != block_order[:, None, None]
    key_blocks = jnp.transpose(keys.reshape(BLOCK_COUNT, BLK, kv_heads, head_dim), (2, 0, 1, 3))
    value_blocks = jnp.transpose(values.reshape(BLOCK_COUNT, BLK, kv_heads, head_dim), (2, 0, 1, 3))
    head_ids = jnp.arange(kv_heads)[:, None]

    def one_block(pieces):
        query_blk, keys_own, values_own, slots_here, ok_here = pieces
        keys_sel = key_blocks[head_ids, slots_here]
        values_sel = value_blocks[head_ids, slots_here]
        return attend_block(query_blk.reshape(BLK, kv_heads, per_group, head_dim), keys_sel, values_sel, ok_here, keys_own, values_own)

    attended = lax.map(one_block, (queries.reshape(BLOCK_COUNT, BLK, q_heads, head_dim), keys.reshape(BLOCK_COUNT, BLK, kv_heads, head_dim), values.reshape(BLOCK_COUNT, BLK, kv_heads, head_dim), chosen_slots, slot_ok))
    attended = attended.reshape(TOKEN_COUNT, q_heads * head_dim)
    return jnp.dot(attended, w_out, preferred_element_type=jnp.float32).astype(jnp.bfloat16)
```

```python
import functools

import jax
import jax.numpy as jnp
from jax import lax
from jax.experimental import pallas as pl
from jax.experimental.pallas import tpu as pltpu
from jax.sharding import PartitionSpec as P

BLK = 512
HEAD = 128
TOPK = 3
PIECE = 16
FACTOR = HEAD ** -0.5
LOG2E = 1.4426950408889634

SWAP_Z = [(0, 2), (2, 0), (1, 3), (3, 1)]
SWAP_CORE = [(0, 1), (1, 0), (2, 3), (3, 2)]


def pack_kernel(slots_ref, held_ref, out_ref):
    n_dst = out_ref.shape[0]

    def body(dst, carry):
        for j in range(TOPK):
            slot = slots_ref[dst * TOPK + j]
            out_ref[dst, j * PIECE : (j + 1) * PIECE, :] = held_ref[slot, :PIECE, :]
        return carry

    lax.fori_loop(0, n_dst, body, 0, unroll=4)


def attend_kernel(ok_ref, q_ref, k_ref, v_ref, got_ref, out_ref, *, rows):
    half = got_ref.shape[0] // 2
    heads = q_ref.shape[0]
    contract = (((1,), (1,)), ((), ()))
    for h in range(heads):
        for r in range(0, BLK, rows):
            q = q_ref[h, r : r + rows, :]
            seen = r + rows
            near = lax.dot_general(q, k_ref[:seen, :], contract, preferred_element_type=jnp.float32)
            row = lax.broadcasted_iota(jnp.int32, near.shape, 0) + r
            col = lax.broadcasted_iota(jnp.int32, near.shape, 1)
            near = jnp.where(col <= row, near, -jnp.inf)
            far = []
            for j in range(TOPK):
                k_j = got_ref[:half, j * PIECE : (j + 1) * PIECE, :].reshape(BLK, HEAD)
                s = lax.dot_general(q, k_j, contract, preferred_element_type=jnp.float32)
                far.append(jnp.where(ok_ref[j] != 0, s, -jnp.inf))
            highest = jnp.max(near, axis=1, keepdims=True)
            for s in far:
                highest = jnp.maximum(highest, jnp.max(s, axis=1, keepdims=True))
            w = jnp.exp2((near - highest) * (FACTOR * LOG2E))
            total = jnp.sum(w, axis=1, keepdims=True)
            acc = jnp.dot(w.astype(jnp.bfloat16), v_ref[:seen, :], preferred_element_type=jnp.float32)
            for j in range(TOPK):
                v_j = got_ref[half:, j * PIECE : (j + 1) * PIECE, :].reshape(BLK, HEAD)
                w = jnp.exp2((far[j] - highest) * (FACTOR * LOG2E))
                total = total + jnp.sum(w, axis=1, keepdims=True)
                acc = acc + jnp.dot(w.astype(jnp.bfloat16), v_j, preferred_element_type=jnp.float32)
            out_ref[r : r + rows, h * HEAD : (h + 1) * HEAD] = (acc / total).astype(jnp.bfloat16)


def local(queries, keys, values, w_out, block_order, chosen):
    n_blocks = block_order.shape[0]
    head_at = lax.axis_index("head")
    z_hi, core = head_at // 2, head_at % 2
    cols = w_out.shape[1] // 4
    bf16 = jnp.bfloat16

    kv = jnp.concatenate([keys[:, 0, :], values[:, 0, :]], axis=0).reshape(n_blocks, PIECE, HEAD)
    picks = jnp.pad(chosen.reshape(1, 1, TOPK).astype(bf16), ((0, 0), (0, PIECE - 1), (0, HEAD - TOPK)))
    picks = jnp.broadcast_to(picks, (n_blocks, PIECE, HEAD))
    held = lax.all_to_all(jnp.concatenate([kv, picks], axis=1), "ctx", 0, 0, tiled=True)

    picked = held[:, PIECE, :TOPK].astype(jnp.int32)
    same = block_order[None, None, :] == picked[:, :, None]
    slots = jnp.sum(jnp.where(same, jnp.arange(n_blocks, dtype=jnp.int32), 0), axis=2).reshape(-1)
    smem = pl.BlockSpec(memory_space=pltpu.SMEM)
    vmem = pl.BlockSpec(memory_space=pltpu.VMEM)
    packed = pl.pallas_call(
        pack_kernel,
        out_shape=jax.ShapeDtypeStruct((n_blocks, TOPK * PIECE, HEAD), bf16),
        in_specs=[smem, vmem],
        out_specs=vmem,
        name="pack",
    )(slots, held)
    got = lax.all_to_all(packed, "ctx", 0, 0, tiled=True)

    far_cols = lax.dynamic_slice_in_dim(w_out, (1 - z_hi) * 2 * cols, 2 * cols, axis=1)
    near_cols = lax.dynamic_slice_in_dim(w_out, z_hi * 2 * cols, 2 * cols, axis=1)
    far_rows = lax.ppermute(far_cols, "head", SWAP_Z)

    def mine(a):
        return lax.dynamic_slice_in_dim(a, core * cols, cols, axis=1)

    def other(a):
        return lax.dynamic_slice_in_dim(a, (1 - core) * cols, cols, axis=1)

    w_own, w_z = mine(near_cols), mine(far_rows)
    w_core = lax.ppermute(other(near_cols), "head", SWAP_CORE)
    w_zc = lax.ppermute(other(far_rows), "head", SWAP_CORE)

    own = lax.dynamic_slice_in_dim(block_order, lax.axis_index("ctx"), 1)
    ok = (chosen[0, 0] != own).astype(jnp.int32)
    q = jnp.transpose(queries, (1, 0, 2))
    a_own = pl.pallas_call(
        functools.partial(attend_kernel, rows=256),
        out_shape=jax.ShapeDtypeStruct((BLK, queries.shape[1] * HEAD), bf16),
        in_specs=[smem, vmem, vmem, vmem, vmem],
        out_specs=vmem,
        compiler_params=pltpu.CompilerParams(vmem_limit_bytes=48 * 1024 * 1024),
        name="attend",
    )(ok, q, keys[:, 0, :], values[:, 0, :], got)

    a_z = lax.ppermute(a_own, "head", SWAP_Z)
    a_core = lax.ppermute(a_own, "head", SWAP_CORE)
    a_zc = lax.ppermute(a_z, "head", SWAP_CORE)
    dot = functools.partial(jnp.dot, preferred_element_type=jnp.float32)
    out = dot(a_own, w_own) + dot(a_core, w_core) + dot(a_z, w_z) + dot(a_zc, w_zc)
    return out.astype(bf16)


def solution(mesh):
    in_specs = (
        P("ctx", "head", None),
        P("ctx", "head", None),
        P("ctx", "head", None),
        P("head", None),
        P(),
        P("ctx", "head", None),
    )
    out_specs = P("ctx", "head")
    return jax.shard_map(local, mesh=mesh, in_specs=in_specs, out_specs=out_specs, check_vma=False)
```

```python
import functools

import jax
import jax.numpy as jnp
from jax import lax
from jax.experimental import pallas as pl
from jax.experimental.pallas import tpu as pltpu
from jax.sharding import PartitionSpec as P

BLK = 512
HEAD = 128
TOPK = 3
PIECE = 16
NOTE = 8
VMEM_MB = 16
FACTOR = HEAD ** -0.5
LOG2E = 1.4426950408889634
PARTS = 2

SWAP_CORE = [(0, 1), (1, 0), (2, 3), (3, 2)]
SWAP_Z = [(0, 2), (2, 0), (1, 3), (3, 1)]


def along_x(step):
    return [(c, c // 16 * 16 + (c // 4 + step) % 4 * 4 + c % 4) for c in range(64)]


def along_y(step):
    return [(c, (c // 16 + step) % 4 * 16 + c % 16) for c in range(64)]


def along_z(step):
    pairs = []
    for xy in range(16):
        for z in range(8):
            to = (z + step) % 8
            for core in range(2):
                pairs.append(((xy * 4 + z % 4) * 4 + z // 4 * 2 + core, (xy * 4 + to % 4) * 4 + to // 4 * 2 + core))
    return pairs


def over_z(a, step):
    for _ in range(2):
        a = lax.ppermute(a, ("ctx", "head"), along_z(step))
    return a


def cut_kernel(w_ref, same_ref, other_ref, sems):
    share, cols = same_ref.shape
    at = lax.axis_index("head")
    row = pl.multiple_of(lax.shift_right_logical(lax.axis_index("ctx"), 2) * share, share)
    rows = pl.ds(row, share)
    same_col = pl.multiple_of(lax.bitwise_xor(at, 2) * cols, cols)
    other_col = pl.multiple_of(lax.bitwise_xor(at, 3) * cols, cols)
    copies = (
        pltpu.make_async_copy(w_ref.at[rows, pl.ds(same_col, cols)], same_ref, sems.at[0]),
        pltpu.make_async_copy(w_ref.at[rows, pl.ds(other_col, cols)], other_ref, sems.at[1]),
    )
    for copy in copies:
        copy.start()
    for copy in copies:
        copy.wait()


def spread_kernel(chosen_ref, k_ref, v_ref, out_ref):
    half = out_ref.shape[0] // 2
    lane = lax.broadcasted_iota(jnp.int32, (NOTE, HEAD), 1)
    note = jnp.where(lane == 0, chosen_ref[0], jnp.where(lane == 1, chosen_ref[1], chosen_ref[2]))
    note = note.astype(jnp.float32).astype(jnp.bfloat16)
    for c in range(half):
        piece = slice(c * PIECE, (c + 1) * PIECE)
        out_ref[c] = jnp.concatenate([k_ref[piece, :], note], axis=0)
        out_ref[half + c] = jnp.concatenate([v_ref[piece, :], note], axis=0)


def pack_kernel(order_ref, picked_ref, held_ref, same_ref, other_ref, out_ref, slot_of):
    n_dst = out_ref.shape[0]
    for s in range(n_dst):
        slot_of[order_ref[s]] = s
    for first in range(0, n_dst, 8):
        todo = [(d, j) for d in range(first, first + 8) for j in range(TOPK)]
        slots = [slot_of[picked_ref[d, j]] for d, j in todo]
        pieces = [held_ref[slot, :PIECE, :] for slot in slots]
        for (d, j), piece in zip(todo, pieces):
            out_ref[d, j * PIECE : (j + 1) * PIECE, :] = piece


def merge_x_kernel(*refs):
    out_ref = refs[-1]
    x = lax.bitwise_and(lax.shift_right_logical(lax.axis_index("ctx"), 2), 3)
    for k in range(4):
        at = lax.bitwise_and(x + (4 - k), 3)
        for a in range(2):
            out_ref[a, at] = refs[k][a]


def weights_kernel(*refs):
    *quarter_refs, w_ref, core_ref, out_ref, sems = refs
    half, cols = core_ref.shape
    y = lax.shift_right_logical(lax.axis_index("ctx"), 4)
    own = pl.ds(pl.multiple_of(lax.axis_index("head") * cols, cols), cols)
    copies = [
        pltpu.make_async_copy(w_ref.at[:, own], out_ref.at[0], sems.at[0]),
        pltpu.make_async_copy(core_ref, out_ref.at[1], sems.at[1]),
    ]
    for copy in copies:
        copy.start()
    for k, ref in enumerate(quarter_refs):
        at = pl.multiple_of(lax.bitwise_and(y + (4 - k), 3) * HEAD, HEAD)
        for a in range(2):
            out_ref[2 + a, pl.ds(at, HEAD), :] = ref[a].reshape(HEAD, cols)
    for copy in copies:
        copy.wait()


def attend_kernel(ok_ref, q_ref, k_ref, v_ref, got_ref, pass_ref, *out_refs, rows):
    out_refs = out_refs[:PARTS]
    half = got_ref.shape[0] // 2
    heads = q_ref.shape[0]
    contract = (((1,), (1,)), ((), ()))
    for h in range(heads):
        for r in range(0, BLK, rows):
            q = q_ref[h, r : r + rows, :]
            seen = r + rows
            near = lax.dot_general(q, k_ref[:seen, :], contract, preferred_element_type=jnp.float32)
            row = lax.broadcasted_iota(jnp.int32, near.shape, 0) + r
            col = lax.broadcasted_iota(jnp.int32, near.shape, 1)
            near = jnp.where(col <= row, near, -jnp.inf)
            far = []
            for j in range(TOPK):
                k_j = got_ref[:half, j * PIECE : (j + 1) * PIECE, :].reshape(BLK, HEAD)
                s = lax.dot_general(q, k_j, contract, preferred_element_type=jnp.float32)
                far.append(jnp.where(ok_ref[j] != 0, s, -jnp.inf))
            highest = jnp.max(near, axis=1, keepdims=True)
            for s in far:
                highest = jnp.maximum(highest, jnp.max(s, axis=1, keepdims=True))
            w = jnp.exp2((near - highest) * (FACTOR * LOG2E))
            total = jnp.sum(w, axis=1, keepdims=True)
            acc = jnp.dot(w.astype(jnp.bfloat16), v_ref[:seen, :], preferred_element_type=jnp.float32)
            for j in range(TOPK):
                v_j = got_ref[half:, j * PIECE : (j + 1) * PIECE, :].reshape(BLK, HEAD)
                w = jnp.exp2((far[j] - highest) * (FACTOR * LOG2E))
                total = total + jnp.sum(w, axis=1, keepdims=True)
                acc = acc + jnp.dot(w.astype(jnp.bfloat16), v_j, preferred_element_type=jnp.float32)
            per = heads // len(out_refs)
            part, col = out_refs[h // per], h % per * HEAD
            part[r : r + rows, col : col + HEAD] = (acc / total).astype(jnp.bfloat16)


def project_kernel(*refs):
    *part_refs, w_ref, out_ref, lhs, sems = refs
    wide = part_refs[0].shape[1]
    copies = [
        pltpu.make_async_copy(ref, lhs.at[i // PARTS, :, i % PARTS * wide : (i % PARTS + 1) * wide], sems.at[i])
        for i, ref in enumerate(part_refs)
    ]
    for copy in copies:
        copy.start()
    total = None
    for i in range(4):
        for copy in copies[i * PARTS : (i + 1) * PARTS]:
            copy.wait()
        product = jnp.dot(lhs[i], w_ref[i], preferred_element_type=jnp.float32)
        total = product if total is None else total + product
    out_ref[...] = total.astype(jnp.bfloat16)


def local(queries, keys, values, w_out, block_order, chosen):
    n_blocks = block_order.shape[0]
    ctx = lax.axis_index("ctx")
    head_at = lax.axis_index("head")
    cols = w_out.shape[1] // 4
    share = BLK // 16
    bf16 = jnp.bfloat16
    smem = pl.BlockSpec(memory_space=pltpu.SMEM)
    vmem = pl.BlockSpec(memory_space=pltpu.VMEM)
    hbm = pl.BlockSpec(memory_space=pl.ANY)
    params = pltpu.CompilerParams(vmem_limit_bytes=VMEM_MB * 1024 * 1024)
    k_own, v_own = keys[:, 0, :], values[:, 0, :]

    piece = jax.ShapeDtypeStruct((share, cols), bf16)
    far_same, far_other = pl.pallas_call(
        cut_kernel,
        out_shape=(piece, piece),
        in_specs=[hbm],
        out_specs=(vmem, vmem),
        scratch_shapes=[pltpu.SemaphoreType.DMA((2,))],
        name="cut",
    )(w_out)
    far_same = lax.ppermute(far_same, "head", SWAP_Z)
    far_other = lax.ppermute(far_other, "head", SWAP_Z)

    spread = pl.pallas_call(
        spread_kernel,
        out_shape=jax.ShapeDtypeStruct((n_blocks, PIECE + NOTE, HEAD), bf16),
        in_specs=[smem, vmem, vmem],
        out_specs=vmem,
        name="spread",
    )(chosen.reshape(TOPK), k_own, v_own)
    held = lax.all_to_all(spread, "ctx", 0, 0, tiled=True)

    both = jnp.stack([far_same, lax.ppermute(far_other, "head", SWAP_CORE)])
    quarter = pl.pallas_call(
        merge_x_kernel,
        out_shape=jax.ShapeDtypeStruct((2, 4, share, cols), bf16),
        in_specs=[vmem] * 4,
        out_specs=vmem,
        name="merge_x",
    )(both, *[lax.ppermute(both, "ctx", along_x(k)) for k in (1, 2, 3)])

    picked = held[:, PIECE, :TOPK].astype(jnp.int32)
    packed = pl.pallas_call(
        pack_kernel,
        out_shape=jax.ShapeDtypeStruct((n_blocks, TOPK * PIECE, HEAD), bf16),
        in_specs=[smem, smem, vmem, hbm, hbm],
        out_specs=vmem,
        scratch_shapes=[pltpu.SMEM((n_blocks,), jnp.int32)],
        name="pack",
    )(block_order, picked, held, far_same, far_other)
    got = lax.all_to_all(packed, "ctx", 0, 0, tiled=True)

    own = lax.dynamic_slice_in_dim(block_order, ctx, 1)
    ok = (chosen[0, 0] != own).astype(jnp.int32)
    q = jnp.transpose(queries, (1, 0, 2))
    part = jax.ShapeDtypeStruct((BLK, 4 // PARTS * HEAD), bf16)
    *a_own, quarter = pl.pallas_call(
        functools.partial(attend_kernel, rows=256),
        out_shape=(part,) * PARTS + (jax.ShapeDtypeStruct(quarter.shape, bf16),),
        in_specs=[smem, vmem, vmem, vmem, vmem, hbm],
        out_specs=(vmem,) * PARTS + (hbm,),
        input_output_aliases={5: PARTS},
        compiler_params=params,
        cost_estimate=pl.CostEstimate(flops=1 << 20, bytes_accessed=1 << 10, transcendentals=0),
        name="attend",
    )(ok, q, k_own, v_own, got, quarter)

    a_z = [over_z(a, step) for a, step in zip(a_own, (2, -2))]
    a_core = [lax.ppermute(a, "head", SWAP_CORE) for a in a_own]
    a_zc = [lax.ppermute(a, "head", SWAP_CORE) for a in a_z]
    w_core = lax.dynamic_slice_in_dim(w_out, lax.bitwise_xor(head_at, 1) * cols, cols, axis=1)
    w_core = lax.ppermute(w_core, "head", SWAP_CORE)
    weights = pl.pallas_call(
        weights_kernel,
        out_shape=jax.ShapeDtypeStruct((4, BLK, cols), bf16),
        in_specs=[vmem] * 4 + [hbm] * 2,
        out_specs=vmem,
        scratch_shapes=[pltpu.SemaphoreType.DMA((2,))],
        compiler_params=params,
        name="weights",
    )(quarter, *[lax.ppermute(quarter, "ctx", along_y(k)) for k in (1, 2, 3)], w_out, w_core)

    return pl.pallas_call(
        project_kernel,
        out_shape=jax.ShapeDtypeStruct((BLK, cols), bf16),
        in_specs=[vmem] * (4 * PARTS) + [vmem],
        out_specs=vmem,
        scratch_shapes=[pltpu.VMEM((4, BLK, 4 * HEAD), bf16), pltpu.SemaphoreType.DMA((4 * PARTS,))],
        compiler_params=params,
        cost_estimate=pl.CostEstimate(flops=1 << 31, bytes_accessed=4 << 20, transcendentals=0),
        name="project",
    )(*a_own, *a_core, *a_z, *a_zc, weights)


def solution(mesh):
    in_specs = (
        P("ctx", "head", None),
        P("ctx", "head", None),
        P("ctx", "head", None),
        P("head", None),
        P(),
        P("ctx", "head", None),
    )
    out_specs = P("ctx", "head")
    return jax.shard_map(local, mesh=mesh, in_specs=in_specs, out_specs=out_specs, check_vma=False)
```

```python
import functools

import jax
import jax.numpy as jnp
from jax import lax
from jax.experimental import pallas as pl
from jax.experimental.pallas import tpu as pltpu
from jax.sharding import PartitionSpec as P

BLK = 512
HEAD = 128
TOPK = 3
PIECE = 16
NOTE = 8
VMEM_MB = 16
FACTOR = HEAD ** -0.5
LOG2E = 1.4426950408889634
CALLS = 1
PARTS = 2

SWAP_CORE = [(0, 1), (1, 0), (2, 3), (3, 2)]
SWAP_Z = [(0, 2), (2, 0), (1, 3), (3, 1)]


def along_x(step):
    return [(c, c // 16 * 16 + (c // 4 + step) % 4 * 4 + c % 4) for c in range(64)]


def along_y(step):
    return [(c, (c // 16 + step) % 4 * 16 + c % 16) for c in range(64)]


def along_z(step):
    pairs = []
    for xy in range(16):
        for z in range(8):
            to = (z + step) % 8
            for core in range(2):
                pairs.append(((xy * 4 + z % 4) * 4 + z // 4 * 2 + core, (xy * 4 + to % 4) * 4 + to // 4 * 2 + core))
    return pairs


def over_z(a, step):
    for _ in range(2):
        a = lax.ppermute(a, ("ctx", "head"), along_z(step))
    return a


def cut_kernel(w_ref, same_ref, other_ref, core_ref, own_ref, sems):
    share, cols = same_ref.shape
    at = lax.axis_index("head")
    row = pl.multiple_of(lax.shift_right_logical(lax.axis_index("ctx"), 2) * share, share)
    rows = pl.ds(row, share)
    same_col = pl.multiple_of(lax.bitwise_xor(at, 2) * cols, cols)
    other_col = pl.multiple_of(lax.bitwise_xor(at, 3) * cols, cols)
    core_col = pl.multiple_of(lax.bitwise_xor(at, 1) * cols, cols)
    copies = (
        pltpu.make_async_copy(w_ref.at[rows, pl.ds(same_col, cols)], same_ref, sems.at[0]),
        pltpu.make_async_copy(w_ref.at[rows, pl.ds(other_col, cols)], other_ref, sems.at[1]),
        pltpu.make_async_copy(w_ref.at[:, pl.ds(core_col, cols)], core_ref, sems.at[2]),
        pltpu.make_async_copy(w_ref.at[:, pl.ds(pl.multiple_of(at * cols, cols), cols)], own_ref, sems.at[3]),
    )
    for copy in copies:
        copy.start()
    for copy in copies:
        copy.wait()


def spread_kernel(order_ref, chosen_ref, k_ref, v_ref, out_ref):
    half = out_ref.shape[0] // 2
    slots = [jnp.int32(0)] * TOPK
    for s in range(out_ref.shape[0]):
        slots = [jnp.where(order_ref[s] == chosen_ref[j], s, slot) for j, slot in enumerate(slots)]
    lane = lax.broadcasted_iota(jnp.int32, (NOTE, HEAD), 1)
    note = jnp.where(lane == 0, slots[0], jnp.where(lane == 1, slots[1], slots[2]))
    note = note.astype(jnp.float32).astype(jnp.bfloat16)
    for c in range(half):
        piece = slice(c * PIECE, (c + 1) * PIECE)
        out_ref[c] = jnp.concatenate([k_ref[piece, :], note], axis=0)
        out_ref[half + c] = jnp.concatenate([v_ref[piece, :], note], axis=0)


def pack_kernel(slots_ref, held_ref, first_ref, second_ref, out_ref):
    n_dst = out_ref.shape[0]
    for first in range(0, n_dst, 8):
        todo = [(d, j) for d in range(first, first + 8) for j in range(TOPK)]
        slots = [slots_ref[d, j] for d, j in todo]
        pieces = [held_ref[slot, :PIECE, :] for slot in slots]
        for (d, j), piece in zip(todo, pieces):
            out_ref[d, j * PIECE : (j + 1) * PIECE, :] = piece


def merge_x_kernel(*refs):
    *piece_refs, out_ref, sems = refs
    x = lax.bitwise_and(lax.shift_right_logical(lax.axis_index("ctx"), 2), 3)
    copies = []
    for k, ref in enumerate(piece_refs):
        at = lax.bitwise_and(x + (4 - k), 3)
        copies.append(pltpu.make_async_copy(ref, out_ref.at[:, at], sems.at[k]))
        copies[-1].start()
    for copy in copies:
        copy.wait()


def weights_kernel(*refs):
    *quarter_refs, out_ref, sems = refs
    y = lax.shift_right_logical(lax.axis_index("ctx"), 4)
    copies = []
    for k, ref in enumerate(quarter_refs):
        at = lax.bitwise_and(y + (4 - k), 3)
        copies.append(pltpu.make_async_copy(ref, out_ref.at[:, at], sems.at[k]))
        copies[-1].start()
    for copy in copies:
        copy.wait()


def attend_kernel(ok_ref, q_ref, k_ref, v_ref, got_ref, pass_ref, *out_refs, rows):
    out_refs = out_refs[:PARTS]
    half = got_ref.shape[0] // 2
    heads = q_ref.shape[0]
    contract = (((1,), (1,)), ((), ()))
    for h in range(heads):
        for r in range(0, BLK, rows):
            q = q_ref[h, r : r + rows, :]
            seen = r + rows
            near = lax.dot_general(q, k_ref[:seen, :], contract, preferred_element_type=jnp.float32)
            row = lax.broadcasted_iota(jnp.int32, near.shape, 0) + r
            col = lax.broadcasted_iota(jnp.int32, near.shape, 1)
            near = jnp.where(col <= row, near, -jnp.inf)
            far = []
            for j in range(TOPK):
                k_j = got_ref[:half, j * PIECE : (j + 1) * PIECE, :].reshape(BLK, HEAD)
                s = lax.dot_general(q, k_j, contract, preferred_element_type=jnp.float32)
                far.append(s)
            highest = jnp.max(near, axis=1, keepdims=True)
            for j, s in enumerate(far):
                here = jnp.max(s, axis=1, keepdims=True)
                highest = jnp.maximum(highest, jnp.where(ok_ref[j] != 0, here, -jnp.inf))
            w = jnp.exp2((near - highest) * (FACTOR * LOG2E))
            total = jnp.sum(w, axis=1, keepdims=True)
            acc = jnp.dot(w.astype(jnp.bfloat16), v_ref[:seen, :], preferred_element_type=jnp.float32)
            for j in range(TOPK):
                v_j = got_ref[half:, j * PIECE : (j + 1) * PIECE, :].reshape(BLK, HEAD)
                w = jnp.exp2((far[j] - jnp.where(ok_ref[j] != 0, highest, jnp.inf)) * (FACTOR * LOG2E))
                total = total + jnp.sum(w, axis=1, keepdims=True)
                acc = acc + jnp.dot(w.astype(jnp.bfloat16), v_j, preferred_element_type=jnp.float32)
            per = heads // len(out_refs)
            part, col = out_refs[h // per], h % per * HEAD
            part[r : r + rows, col : col + HEAD] = (acc / total).astype(jnp.bfloat16)


def fetch(part_refs, lhs, sems):
    wide = part_refs[0].shape[1]
    copies = [
        pltpu.make_async_copy(ref, lhs.at[:, i * wide : (i + 1) * wide], sems.at[i]) for i, ref in enumerate(part_refs)
    ]
    for copy in copies:
        copy.start()
    return copies


def near_kernel(*refs):
    *part_refs, own_ref, core_ref, out_ref, lhs, sems = refs
    for copy in fetch(part_refs, lhs, sems):
        copy.wait()
    half = own_ref.shape[0]
    out_ref[...] = jnp.dot(lhs[:, :half], own_ref[...], preferred_element_type=jnp.float32) + jnp.dot(
        lhs[:, half:], core_ref[...], preferred_element_type=jnp.float32
    )


def last_kernel(*refs):
    *part_refs, w_ref, near_ref, out_ref, lhs, sems = refs
    copies = fetch(part_refs, lhs, sems)
    for copy in copies:
        copy.wait()
    w = w_ref[...].reshape(lhs.shape[1], -1)
    far = jnp.dot(lhs[...], w, preferred_element_type=jnp.float32)
    out_ref[...] = (near_ref[...] + far).astype(jnp.bfloat16)


def local(queries, keys, values, w_out, block_order, chosen):
    n_blocks = block_order.shape[0]
    ctx = lax.axis_index("ctx")
    head_at = lax.axis_index("head")
    cols = w_out.shape[1] // 4
    share = BLK // 16
    bf16 = jnp.bfloat16
    smem = pl.BlockSpec(memory_space=pltpu.SMEM)
    vmem = pl.BlockSpec(memory_space=pltpu.VMEM)
    hbm = pl.BlockSpec(memory_space=pl.ANY)
    stay = pl.BlockSpec(memory_space=pltpu.HBM)
    params = pltpu.CompilerParams(vmem_limit_bytes=VMEM_MB * 1024 * 1024)
    k_own, v_own = keys[:, 0, :], values[:, 0, :]

    piece = jax.ShapeDtypeStruct((share, cols), bf16)
    near_rows = jax.ShapeDtypeStruct((BLK, cols), bf16)
    far_same, far_other, w_core, w_own = pl.pallas_call(
        cut_kernel,
        out_shape=(piece, piece, near_rows, near_rows),
        in_specs=[stay],
        out_specs=(vmem,) * 4,
        scratch_shapes=[pltpu.SemaphoreType.DMA((4,))],
        name="cut",
    )(w_out)
    far_same = lax.ppermute(far_same, "head", SWAP_Z)
    far_other = lax.ppermute(far_other, "head", SWAP_Z)

    spread = pl.pallas_call(
        spread_kernel,
        out_shape=jax.ShapeDtypeStruct((n_blocks, PIECE + NOTE, HEAD), bf16),
        in_specs=[smem, smem, vmem, vmem],
        out_specs=vmem,
        name="spread",
    )(block_order, chosen.reshape(TOPK), k_own, v_own)
    held = lax.all_to_all(spread, "ctx", 0, 0, tiled=True)

    both = jnp.stack([far_same, lax.ppermute(far_other, "head", SWAP_CORE)])
    quarter = pl.pallas_call(
        merge_x_kernel,
        out_shape=jax.ShapeDtypeStruct((2, 4, share, cols), bf16),
        in_specs=[hbm] * 4,
        out_specs=vmem,
        scratch_shapes=[pltpu.SemaphoreType.DMA((4,))],
        name="merge_x",
    )(both, *[lax.ppermute(both, "ctx", along_x(k)) for k in (1, 2, 3)])

    slots = held[:, PIECE, :TOPK].astype(jnp.int32)
    packed = pl.pallas_call(
        pack_kernel,
        out_shape=jax.ShapeDtypeStruct((n_blocks, TOPK * PIECE, HEAD), bf16),
        in_specs=[smem, vmem, hbm, hbm],
        out_specs=vmem,
        name="pack",
    )(slots, held, far_same, far_other)
    got = lax.all_to_all(packed, "ctx", 0, 0, tiled=True)

    own = lax.dynamic_slice_in_dim(block_order, ctx, 1)
    ok = (chosen[0, 0] != own).astype(jnp.int32)
    q = jnp.transpose(queries, (1, 0, 2))
    part = jax.ShapeDtypeStruct((BLK, HEAD * 4 // (CALLS * PARTS)), bf16)
    a_own, a_z = [], []
    for call in range(CALLS):
        heads = slice(call * 4 // CALLS, (call + 1) * 4 // CALLS)
        *parts, quarter = pl.pallas_call(
            functools.partial(attend_kernel, rows=256),
            out_shape=(part,) * PARTS + (jax.ShapeDtypeStruct(quarter.shape, bf16),),
            in_specs=[smem, vmem, vmem, vmem, vmem, hbm],
            out_specs=(vmem,) * PARTS + (hbm,),
            input_output_aliases={5: PARTS},
            compiler_params=params,
            cost_estimate=pl.CostEstimate(flops=1 << 20, bytes_accessed=1 << 10, transcendentals=0),
            name="attend",
        )(ok, q[heads], k_own, v_own, got, quarter)
        a_own += parts
        a_z += [over_z(a, step) for a, step in zip(parts, (2, -2))]
    a_core = [lax.ppermute(a, "head", SWAP_CORE) for a in a_own]
    a_zc = [lax.ppermute(a, "head", SWAP_CORE) for a in a_z]

    w_far = pl.pallas_call(
        weights_kernel,
        out_shape=jax.ShapeDtypeStruct((2, 4, 4, share, cols), bf16),
        in_specs=[hbm] * 4,
        out_specs=vmem,
        scratch_shapes=[pltpu.SemaphoreType.DMA((4,))],
        compiler_params=params,
        name="weights",
    )(quarter, *[lax.ppermute(quarter, "ctx", along_y(k)) for k in (1, 2, 3)])
    w_core = lax.ppermute(w_core, "head", SWAP_CORE)
    lhs = pltpu.VMEM((BLK, 8 * HEAD), bf16)
    near = pl.pallas_call(
        near_kernel,
        out_shape=jax.ShapeDtypeStruct((BLK, cols), jnp.float32),
        in_specs=[hbm] * (2 * len(a_own)) + [vmem] * 2,
        out_specs=vmem,
        scratch_shapes=[lhs, pltpu.SemaphoreType.DMA((2 * len(a_own),))],
        compiler_params=params,
        name="near",
    )(*a_own, *a_core, w_own, w_core)
    return pl.pallas_call(
        last_kernel,
        out_shape=jax.ShapeDtypeStruct((BLK, cols), bf16),
        in_specs=[hbm] * (2 * len(a_own)) + [vmem] * 2,
        out_specs=vmem,
        scratch_shapes=[lhs, pltpu.SemaphoreType.DMA((2 * len(a_own),))],
        compiler_params=params,
        name="last",
    )(*a_z, *a_zc, w_far, near)


def solution(mesh):
    in_specs = (
        P("ctx", "head", None),
        P("ctx", "head", None),
        P("ctx", "head", None),
        P("head", None),
        P(),
        P("ctx", "head", None),
    )
    out_specs = P("ctx", "head")
    return jax.shard_map(local, mesh=mesh, in_specs=in_specs, out_specs=out_specs, check_vma=False)
```

```python
import functools

import jax
import jax.numpy as jnp
from jax import lax
from jax.experimental import pallas as pl
from jax.experimental.pallas import tpu as pltpu
from jax.sharding import PartitionSpec as P

BLK = 512
HEAD = 128
TOPK = 3
PIECE = 16
NOTE = 8
VMEM_MB = 16
FACTOR = HEAD ** -0.5
LOG2E = 1.4426950408889634
CALLS = 1
TOGETHER = 2
PARTS = 2

SWAP_CORE = [(0, 1), (1, 0), (2, 3), (3, 2)]
SWAP_Z = [(0, 2), (2, 0), (1, 3), (3, 1)]


def along_x(step):
    return [(c, c // 16 * 16 + (c // 4 + step) % 4 * 4 + c % 4) for c in range(64)]


def along_y(step):
    return [(c, (c // 16 + step) % 4 * 16 + c % 16) for c in range(64)]


def along_z(step):
    pairs = []
    for xy in range(16):
        for z in range(8):
            to = (z + step) % 8
            for core in range(2):
                pairs.append(((xy * 4 + z % 4) * 4 + z // 4 * 2 + core, (xy * 4 + to % 4) * 4 + to // 4 * 2 + core))
    return pairs


def over_z(a, step):
    for _ in range(2):
        a = lax.ppermute(a, ("ctx", "head"), along_z(step))
    return a


def cut_kernel(w_ref, same_ref, other_ref, core_ref, own_ref, sems):
    share, cols = same_ref.shape
    at = lax.axis_index("head")
    row = pl.multiple_of(lax.shift_right_logical(lax.axis_index("ctx"), 2) * share, share)
    rows = pl.ds(row, share)
    same_col = pl.multiple_of(lax.bitwise_xor(at, 2) * cols, cols)
    other_col = pl.multiple_of(lax.bitwise_xor(at, 3) * cols, cols)
    core_col = pl.multiple_of(lax.bitwise_xor(at, 1) * cols, cols)
    copies = (
        pltpu.make_async_copy(w_ref.at[rows, pl.ds(same_col, cols)], same_ref, sems.at[0]),
        pltpu.make_async_copy(w_ref.at[rows, pl.ds(other_col, cols)], other_ref, sems.at[1]),
        pltpu.make_async_copy(w_ref.at[:, pl.ds(core_col, cols)], core_ref, sems.at[2]),
        pltpu.make_async_copy(w_ref.at[:, pl.ds(pl.multiple_of(at * cols, cols), cols)], own_ref, sems.at[3]),
    )
    for copy in copies:
        copy.start()
    for copy in copies:
        copy.wait()


def spread_kernel(order_ref, chosen_ref, k_ref, v_ref, out_ref):
    half = out_ref.shape[0] // 2
    slots = [jnp.int32(0)] * TOPK
    for s in range(out_ref.shape[0]):
        slots = [jnp.where(order_ref[s] == chosen_ref[j], s, slot) for j, slot in enumerate(slots)]
    lane = lax.broadcasted_iota(jnp.int32, (NOTE, HEAD), 1)
    note = jnp.where(lane == 0, slots[0], jnp.where(lane == 1, slots[1], slots[2]))
    note = note.astype(jnp.float32).astype(jnp.bfloat16)
    for c in range(half):
        piece = slice(c * PIECE, (c + 1) * PIECE)
        out_ref[c] = jnp.concatenate([k_ref[piece, :], note], axis=0)
        out_ref[half + c] = jnp.concatenate([v_ref[piece, :], note], axis=0)


def pack_kernel(slots_ref, held_ref, first_ref, second_ref, out_ref):
    n_dst = out_ref.shape[0]
    for first in range(0, n_dst, 8):
        todo = [(d, j) for d in range(first, first + 8) for j in range(TOPK)]
        slots = [slots_ref[d, j] for d, j in todo]
        pieces = [held_ref[slot, :PIECE, :] for slot in slots]
        for (d, j), piece in zip(todo, pieces):
            out_ref[d, j * PIECE : (j + 1) * PIECE, :] = piece


def merge_x_kernel(*refs):
    *piece_refs, out_ref, sems = refs
    x = lax.bitwise_and(lax.shift_right_logical(lax.axis_index("ctx"), 2), 3)
    copies = []
    for k, ref in enumerate(piece_refs):
        at = lax.bitwise_and(x + (4 - k), 3)
        copies.append(pltpu.make_async_copy(ref, out_ref.at[:, at], sems.at[k]))
        copies[-1].start()
    for copy in copies:
        copy.wait()


def attend_kernel(ok_ref, q_ref, k_ref, v_ref, got_ref, pass_ref, *out_refs, rows):
    out_refs = out_refs[:PARTS]
    half = got_ref.shape[0] // 2
    heads = q_ref.shape[0]
    contract = (((1,), (1,)), ((), ()))
    tiles = [(h, r) for h in range(heads) for r in range(0, BLK, rows)]
    for first in range(0, len(tiles), TOGETHER):
        group = tiles[first : first + TOGETHER]
        scores = []
        for h, r in group:
            q = q_ref[h, r : r + rows, :]
            near = lax.dot_general(q, k_ref[: r + rows, :], contract, preferred_element_type=jnp.float32)
            row = lax.broadcasted_iota(jnp.int32, near.shape, 0) + r
            col = lax.broadcasted_iota(jnp.int32, near.shape, 1)
            near = jnp.where(col <= row, near, -jnp.inf)
            far = []
            for j in range(TOPK):
                k_j = got_ref[:half, j * PIECE : (j + 1) * PIECE, :].reshape(BLK, HEAD)
                far.append(lax.dot_general(q, k_j, contract, preferred_element_type=jnp.float32))
            scores.append((near, far))
        for (h, r), (near, far) in zip(group, scores):
            highest = jnp.max(near, axis=1, keepdims=True)
            for j, s in enumerate(far):
                here = jnp.max(s, axis=1, keepdims=True)
                highest = jnp.maximum(highest, jnp.where(ok_ref[j] != 0, here, -jnp.inf))
            w = jnp.exp2((near - highest) * (FACTOR * LOG2E))
            total = jnp.sum(w, axis=1, keepdims=True)
            acc = jnp.dot(w.astype(jnp.bfloat16), v_ref[: r + rows, :], preferred_element_type=jnp.float32)
            for j in range(TOPK):
                v_j = got_ref[half:, j * PIECE : (j + 1) * PIECE, :].reshape(BLK, HEAD)
                w = jnp.exp2((far[j] - jnp.where(ok_ref[j] != 0, highest, jnp.inf)) * (FACTOR * LOG2E))
                total = total + jnp.sum(w, axis=1, keepdims=True)
                acc = acc + jnp.dot(w.astype(jnp.bfloat16), v_j, preferred_element_type=jnp.float32)
            per = heads // len(out_refs)
            part, col = out_refs[h // per], h % per * HEAD
            part[r : r + rows, col : col + HEAD] = (acc / total).astype(jnp.bfloat16)


def fetch(part_refs, lhs, sems):
    wide = part_refs[0].shape[1]
    copies = [
        pltpu.make_async_copy(ref, lhs.at[:, i * wide : (i + 1) * wide], sems.at[i]) for i, ref in enumerate(part_refs)
    ]
    for copy in copies:
        copy.start()
    return copies


def near_kernel(*refs):
    *part_refs, own_ref, core_ref, out_ref, lhs, sems = refs
    for copy in fetch(part_refs, lhs, sems):
        copy.wait()
    half = own_ref.shape[0]
    out_ref[...] = jnp.dot(lhs[:, :half], own_ref[...], preferred_element_type=jnp.float32) + jnp.dot(
        lhs[:, half:], core_ref[...], preferred_element_type=jnp.float32
    )


def last_kernel(*refs):
    *data_refs, near_ref, out_ref, lhs, w_far, sems = refs
    part_refs, quarter_refs = data_refs[:-4], data_refs[-4:]
    y = lax.shift_right_logical(lax.axis_index("ctx"), 4)
    copies = []
    for k, ref in enumerate(quarter_refs):
        at = lax.bitwise_and(y + (4 - k), 3)
        copies.append(pltpu.make_async_copy(ref, w_far.at[:, at], sems.at[len(part_refs) + k]))
        copies[-1].start()
    for copy in fetch(part_refs, lhs, sems) + copies:
        copy.wait()
    w = w_far[...].reshape(lhs.shape[1], -1)
    far = jnp.dot(lhs[...], w, preferred_element_type=jnp.float32)
    out_ref[...] = (near_ref[...] + far).astype(jnp.bfloat16)


def local(queries, keys, values, w_out, block_order, chosen):
    n_blocks = block_order.shape[0]
    ctx = lax.axis_index("ctx")
    head_at = lax.axis_index("head")
    cols = w_out.shape[1] // 4
    share = BLK // 16
    bf16 = jnp.bfloat16
    smem = pl.BlockSpec(memory_space=pltpu.SMEM)
    vmem = pl.BlockSpec(memory_space=pltpu.VMEM)
    hbm = pl.BlockSpec(memory_space=pl.ANY)
    stay = pl.BlockSpec(memory_space=pltpu.HBM)
    params = pltpu.CompilerParams(vmem_limit_bytes=VMEM_MB * 1024 * 1024)
    k_own, v_own = keys[:, 0, :], values[:, 0, :]

    piece = jax.ShapeDtypeStruct((share, cols), bf16)
    near_rows = jax.ShapeDtypeStruct((BLK, cols), bf16)
    far_same, far_other, w_core, w_own = pl.pallas_call(
        cut_kernel,
        out_shape=(piece, piece, near_rows, near_rows),
        in_specs=[stay],
        out_specs=(vmem,) * 4,
        scratch_shapes=[pltpu.SemaphoreType.DMA((4,))],
        name="cut",
    )(w_out)
    far_same = lax.ppermute(far_same, "head", SWAP_Z)
    far_other = lax.ppermute(far_other, "head", SWAP_Z)

    spread = pl.pallas_call(
        spread_kernel,
        out_shape=jax.ShapeDtypeStruct((n_blocks, PIECE + NOTE, HEAD), bf16),
        in_specs=[smem, smem, vmem, vmem],
        out_specs=vmem,
        name="spread",
    )(block_order, chosen.reshape(TOPK), k_own, v_own)
    held = lax.all_to_all(spread, "ctx", 0, 0, tiled=True)

    both = jnp.stack([far_same, lax.ppermute(far_other, "head", SWAP_CORE)])
    quarter = pl.pallas_call(
        merge_x_kernel,
        out_shape=jax.ShapeDtypeStruct((2, 4, share, cols), bf16),
        in_specs=[hbm] * 4,
        out_specs=vmem,
        scratch_shapes=[pltpu.SemaphoreType.DMA((4,))],
        name="merge_x",
    )(both, *[lax.ppermute(both, "ctx", along_x(k)) for k in (1, 2, 3)])

    slots = held[:, PIECE, :TOPK].astype(jnp.int32)
    packed = pl.pallas_call(
        pack_kernel,
        out_shape=jax.ShapeDtypeStruct((n_blocks, TOPK * PIECE, HEAD), bf16),
        in_specs=[smem, vmem, hbm, hbm],
        out_specs=vmem,
        name="pack",
    )(slots, held, far_same, far_other)
    got = lax.all_to_all(packed, "ctx", 0, 0, tiled=True)

    own = lax.dynamic_slice_in_dim(block_order, ctx, 1)
    ok = (chosen[0, 0] != own).astype(jnp.int32)
    q = jnp.transpose(queries, (1, 0, 2))
    part = jax.ShapeDtypeStruct((BLK, HEAD * 4 // (CALLS * PARTS)), bf16)
    a_own, a_z = [], []
    for call in range(CALLS):
        heads = slice(call * 4 // CALLS, (call + 1) * 4 // CALLS)
        *parts, quarter = pl.pallas_call(
            functools.partial(attend_kernel, rows=256),
            out_shape=(part,) * PARTS + (jax.ShapeDtypeStruct(quarter.shape, bf16),),
            in_specs=[smem, vmem, vmem, vmem, vmem, hbm],
            out_specs=(vmem,) * PARTS + (hbm,),
            input_output_aliases={5: PARTS},
            compiler_params=params,
            cost_estimate=pl.CostEstimate(flops=1 << 20, bytes_accessed=1 << 10, transcendentals=0),
            name="attend",
        )(ok, q[heads], k_own, v_own, got, quarter)
        a_own += parts
        a_z += [over_z(a, step) for a, step in zip(parts, (2, -2))]
    a_core = [lax.ppermute(a, "head", SWAP_CORE) for a in a_own]
    a_zc = [lax.ppermute(a, "head", SWAP_CORE) for a in a_z]

    quarters = [quarter] + [lax.ppermute(quarter, "ctx", along_y(k)) for k in (1, 2, 3)]
    w_core = lax.ppermute(w_core, "head", SWAP_CORE)
    lhs = pltpu.VMEM((BLK, 8 * HEAD), bf16)
    near = pl.pallas_call(
        near_kernel,
        out_shape=jax.ShapeDtypeStruct((BLK, cols), jnp.float32),
        in_specs=[hbm] * (2 * len(a_own)) + [vmem] * 2,
        out_specs=vmem,
        scratch_shapes=[lhs, pltpu.SemaphoreType.DMA((2 * len(a_own),))],
        compiler_params=params,
        name="near",
    )(*a_own, *a_core, w_own, w_core)
    return pl.pallas_call(
        last_kernel,
        out_shape=jax.ShapeDtypeStruct((BLK, cols), bf16),
        in_specs=[hbm] * (2 * len(a_own) + 4) + [vmem],
        out_specs=vmem,
        scratch_shapes=[
            lhs,
            pltpu.VMEM((2, 4, 4, share, cols), bf16),
            pltpu.SemaphoreType.DMA((2 * len(a_own) + 4,)),
        ],
        compiler_params=params,
        name="last",
    )(*a_z, *a_zc, *quarters, near)


def solution(mesh):
    in_specs = (
        P("ctx", "head", None),
        P("ctx", "head", None),
        P("ctx", "head", None),
        P("head", None),
        P(),
        P("ctx", "head", None),
    )
    out_specs = P("ctx", "head")
    return jax.shard_map(local, mesh=mesh, in_specs=in_specs, out_specs=out_specs, check_vma=False)
```

```python
import functools

import jax
import jax.numpy as jnp
from jax import lax
from jax.experimental import pallas as pl
from jax.experimental.pallas import tpu as pltpu
from jax.sharding import PartitionSpec as P

BLK = 512
HEAD = 128
TOPK = 3
PIECE = 16
NOTE = 8
VMEM_MB = 16
FACTOR = HEAD ** -0.5
LOG2E = 1.4426950408889634
CALLS = 1
TOGETHER = 2
PARTS = 2

SWAP_CORE = [(0, 1), (1, 0), (2, 3), (3, 2)]
SWAP_Z = [(0, 2), (2, 0), (1, 3), (3, 1)]


def along_x(step):
    return [(c, c // 16 * 16 + (c // 4 + step) % 4 * 4 + c % 4) for c in range(64)]


def along_y(step):
    return [(c, (c // 16 + step) % 4 * 16 + c % 16) for c in range(64)]


def along_z(step):
    pairs = []
    for xy in range(16):
        for z in range(8):
            to = (z + step) % 8
            for core in range(2):
                pairs.append(((xy * 4 + z % 4) * 4 + z // 4 * 2 + core, (xy * 4 + to % 4) * 4 + to // 4 * 2 + core))
    return pairs


def over_z(a, step):
    for _ in range(2):
        a = lax.ppermute(a, ("ctx", "head"), along_z(step))
    return a


def cut_kernel(w_ref, same_ref, other_ref, core_ref, own_ref, sems):
    share, cols = same_ref.shape
    at = lax.axis_index("head")
    row = pl.multiple_of(lax.shift_right_logical(lax.axis_index("ctx"), 2) * share, share)
    rows = pl.ds(row, share)
    same_col = pl.multiple_of(lax.bitwise_xor(at, 2) * cols, cols)
    other_col = pl.multiple_of(lax.bitwise_xor(at, 3) * cols, cols)
    core_col = pl.multiple_of(lax.bitwise_xor(at, 1) * cols, cols)
    copies = (
        pltpu.make_async_copy(w_ref.at[rows, pl.ds(same_col, cols)], same_ref, sems.at[0]),
        pltpu.make_async_copy(w_ref.at[rows, pl.ds(other_col, cols)], other_ref, sems.at[1]),
        pltpu.make_async_copy(w_ref.at[:, pl.ds(core_col, cols)], core_ref, sems.at[2]),
        pltpu.make_async_copy(w_ref.at[:, pl.ds(pl.multiple_of(at * cols, cols), cols)], own_ref, sems.at[3]),
    )
    for copy in copies:
        copy.start()
    for copy in copies:
        copy.wait()


def spread_kernel(order_ref, chosen_ref, k_ref, v_ref, out_ref):
    half = out_ref.shape[0] // 2
    slots = [jnp.int32(0)] * TOPK
    for s in range(out_ref.shape[0]):
        slots = [jnp.where(order_ref[s] == chosen_ref[j], s, slot) for j, slot in enumerate(slots)]
    lane = lax.broadcasted_iota(jnp.int32, (NOTE, HEAD), 1)
    note = jnp.where(lane == 0, slots[0], jnp.where(lane == 1, slots[1], slots[2]))
    note = note.astype(jnp.float32).astype(jnp.bfloat16)
    for c in range(half):
        piece = slice(c * PIECE, (c + 1) * PIECE)
        out_ref[c] = jnp.concatenate([k_ref[piece, :], note], axis=0)
        out_ref[half + c] = jnp.concatenate([v_ref[piece, :], note], axis=0)


def pack_kernel(slots_ref, held_ref, first_ref, second_ref, out_ref):
    n_dst = out_ref.shape[0]
    for first in range(0, n_dst, 8):
        todo = [(d, j) for d in range(first, first + 8) for j in range(TOPK)]
        slots = [slots_ref[d, j] for d, j in todo]
        pieces = [held_ref[slot, :PIECE, :] for slot in slots]
        for (d, j), piece in zip(todo, pieces):
            out_ref[d, j * PIECE : (j + 1) * PIECE, :] = piece


def merge_x_kernel(*refs):
    *piece_refs, out_ref, sems = refs
    x = lax.bitwise_and(lax.shift_right_logical(lax.axis_index("ctx"), 2), 3)
    copies = []
    for k, ref in enumerate(piece_refs):
        at = lax.bitwise_and(x + (4 - k), 3)
        copies.append(pltpu.make_async_copy(ref, out_ref.at[:, at], sems.at[k]))
        copies[-1].start()
    for copy in copies:
        copy.wait()


def attend_kernel(ok_ref, q_ref, k_ref, v_ref, got_ref, pass_ref, *out_refs, rows):
    out_refs = out_refs[:PARTS]
    half = got_ref.shape[0] // 2
    heads = q_ref.shape[0]
    contract = (((1,), (1,)), ((), ()))
    tiles = [(h, r) for h in range(heads) for r in range(0, BLK, rows)]
    for first in range(0, len(tiles), TOGETHER):
        group = tiles[first : first + TOGETHER]
        scores = []
        for h, r in group:
            q = q_ref[h, r : r + rows, :]
            near = lax.dot_general(q, k_ref[: r + rows, :], contract, preferred_element_type=jnp.float32)
            row = lax.broadcasted_iota(jnp.int32, near.shape, 0) + r
            col = lax.broadcasted_iota(jnp.int32, near.shape, 1)
            near = jnp.where(col <= row, near, -jnp.inf)
            far = []
            for j in range(TOPK):
                k_j = got_ref[:half, j * PIECE : (j + 1) * PIECE, :].reshape(BLK, HEAD)
                far.append(lax.dot_general(q, k_j, contract, preferred_element_type=jnp.float32))
            scores.append((near, far))
        for (h, r), (near, far) in zip(group, scores):
            highest = jnp.max(near, axis=1, keepdims=True)
            for j, s in enumerate(far):
                here = jnp.max(s, axis=1, keepdims=True)
                highest = jnp.maximum(highest, jnp.where(ok_ref[j] != 0, here, -jnp.inf))
            w = jnp.exp2((near - highest) * (FACTOR * LOG2E))
            total = jnp.sum(w, axis=1, keepdims=True)
            acc = jnp.dot(w.astype(jnp.bfloat16), v_ref[: r + rows, :], preferred_element_type=jnp.float32)
            for j in range(TOPK):
                v_j = got_ref[half:, j * PIECE : (j + 1) * PIECE, :].reshape(BLK, HEAD)
                w = jnp.exp2((far[j] - jnp.where(ok_ref[j] != 0, highest, jnp.inf)) * (FACTOR * LOG2E))
                total = total + jnp.sum(w, axis=1, keepdims=True)
                acc = acc + jnp.dot(w.astype(jnp.bfloat16), v_j, preferred_element_type=jnp.float32)
            per = heads // len(out_refs)
            part, col = out_refs[h // per], h % per * HEAD
            part[r : r + rows, col : col + HEAD] = (acc / total).astype(jnp.bfloat16)


def fetch(part_refs, lhs, sems):
    wide = part_refs[0].shape[1]
    copies = [
        pltpu.make_async_copy(ref, lhs.at[:, i * wide : (i + 1) * wide], sems.at[i]) for i, ref in enumerate(part_refs)
    ]
    for copy in copies:
        copy.start()
    return copies


def near_kernel(*refs):
    *part_refs, own_ref, core_ref, out_ref, lhs, sems = refs
    for copy in fetch(part_refs, lhs, sems):
        copy.wait()
    half = own_ref.shape[0]
    out_ref[...] = jnp.dot(lhs[:, :half], own_ref[...], preferred_element_type=jnp.float32) + jnp.dot(
        lhs[:, half:], core_ref[...], preferred_element_type=jnp.float32
    )


def last_kernel(*refs):
    *data_refs, near_ref, out_ref, lhs, w_far, result, sems = refs
    part_refs, quarter_refs = data_refs[:-4], data_refs[-4:]
    parts = len(part_refs)
    y = lax.shift_right_logical(lax.axis_index("ctx"), 4)
    sides = [[], []]
    for side in range(2):
        for k, ref in enumerate(quarter_refs):
            at = lax.bitwise_and(y + (4 - k), 3)
            sem = sems.at[parts + 4 * side + k]
            sides[side].append(pltpu.make_async_copy(ref.at[side], w_far.at[side, at], sem))
    for copy in sides[0]:
        copy.start()
    copies = fetch(part_refs, lhs, sems)
    for copy in sides[1]:
        copy.start()
    half = lhs.shape[1] // 2
    for copy in copies[: parts // 2] + sides[0]:
        copy.wait()
    first = jnp.dot(lhs[:, :half], w_far[0].reshape(half, -1), preferred_element_type=jnp.float32)
    first = near_ref[...] + first
    for copy in copies[parts // 2 :] + sides[1]:
        copy.wait()
    w = w_far[1].reshape(half, -1)
    sends = []
    for i in range(2):
        rows = slice(i * BLK // 2, (i + 1) * BLK // 2)
        second = jnp.dot(lhs[rows, half:], w, preferred_element_type=jnp.float32)
        result[rows, :] = (first[rows, :] + second).astype(jnp.bfloat16)
        sends.append(pltpu.make_async_copy(result.at[rows, :], out_ref.at[rows, :], sems.at[parts + 8 + i]))
        sends[-1].start()
    for send in sends:
        send.wait()


def local(queries, keys, values, w_out, block_order, chosen):
    n_blocks = block_order.shape[0]
    ctx = lax.axis_index("ctx")
    head_at = lax.axis_index("head")
    cols = w_out.shape[1] // 4
    share = BLK // 16
    bf16 = jnp.bfloat16
    smem = pl.BlockSpec(memory_space=pltpu.SMEM)
    vmem = pl.BlockSpec(memory_space=pltpu.VMEM)
    hbm = pl.BlockSpec(memory_space=pl.ANY)
    stay = pl.BlockSpec(memory_space=pltpu.HBM)
    params = pltpu.CompilerParams(vmem_limit_bytes=VMEM_MB * 1024 * 1024)
    k_own, v_own = keys[:, 0, :], values[:, 0, :]

    piece = jax.ShapeDtypeStruct((share, cols), bf16)
    near_rows = jax.ShapeDtypeStruct((BLK, cols), bf16)
    far_same, far_other, w_core, w_own = pl.pallas_call(
        cut_kernel,
        out_shape=(piece, piece, near_rows, near_rows),
        in_specs=[stay],
        out_specs=(vmem,) * 4,
        scratch_shapes=[pltpu.SemaphoreType.DMA((4,))],
        name="cut",
    )(w_out)
    far_same = lax.ppermute(far_same, "head", SWAP_Z)
    far_other = lax.ppermute(far_other, "head", SWAP_Z)

    spread = pl.pallas_call(
        spread_kernel,
        out_shape=jax.ShapeDtypeStruct((n_blocks, PIECE + NOTE, HEAD), bf16),
        in_specs=[smem, smem, vmem, vmem],
        out_specs=vmem,
        name="spread",
    )(block_order, chosen.reshape(TOPK), k_own, v_own)
    held = lax.all_to_all(spread, "ctx", 0, 0, tiled=True)

    both = jnp.stack([far_same, lax.ppermute(far_other, "head", SWAP_CORE)])
    quarter = pl.pallas_call(
        merge_x_kernel,
        out_shape=jax.ShapeDtypeStruct((2, 4, share, cols), bf16),
        in_specs=[hbm] * 4,
        out_specs=vmem,
        scratch_shapes=[pltpu.SemaphoreType.DMA((4,))],
        name="merge_x",
    )(both, *[lax.ppermute(both, "ctx", along_x(k)) for k in (1, 2, 3)])

    slots = held[:, PIECE, :TOPK].astype(jnp.int32)
    packed = pl.pallas_call(
        pack_kernel,
        out_shape=jax.ShapeDtypeStruct((n_blocks, TOPK * PIECE, HEAD), bf16),
        in_specs=[smem, vmem, hbm, hbm],
        out_specs=vmem,
        name="pack",
    )(slots, held, far_same, far_other)
    got = lax.all_to_all(packed, "ctx", 0, 0, tiled=True)

    own = lax.dynamic_slice_in_dim(block_order, ctx, 1)
    ok = (chosen[0, 0] != own).astype(jnp.int32)
    q = jnp.transpose(queries, (1, 0, 2))
    part = jax.ShapeDtypeStruct((BLK, HEAD * 4 // (CALLS * PARTS)), bf16)
    a_own, a_z = [], []
    for call in range(CALLS):
        heads = slice(call * 4 // CALLS, (call + 1) * 4 // CALLS)
        *parts, quarter = pl.pallas_call(
            functools.partial(attend_kernel, rows=256),
            out_shape=(part,) * PARTS + (jax.ShapeDtypeStruct(quarter.shape, bf16),),
            in_specs=[smem, vmem, vmem, vmem, vmem, hbm],
            out_specs=(vmem,) * PARTS + (hbm,),
            input_output_aliases={5: PARTS},
            compiler_params=params,
            cost_estimate=pl.CostEstimate(flops=1 << 20, bytes_accessed=1 << 10, transcendentals=0),
            name="attend",
        )(ok, q[heads], k_own, v_own, got, quarter)
        a_own += parts
        a_z += [over_z(a, step) for a, step in zip(parts, (2, -2))]
    a_core = [lax.ppermute(a, "head", SWAP_CORE) for a in a_own]
    a_zc = [lax.ppermute(a, "head", SWAP_CORE) for a in a_z]

    quarters = [quarter] + [lax.ppermute(quarter, "ctx", along_y(k)) for k in (1, 2, 3)]
    w_core = lax.ppermute(w_core, "head", SWAP_CORE)
    lhs = pltpu.VMEM((BLK, 8 * HEAD), bf16)
    near = pl.pallas_call(
        near_kernel,
        out_shape=jax.ShapeDtypeStruct((BLK, cols), jnp.float32),
        in_specs=[hbm] * (2 * len(a_own)) + [vmem] * 2,
        out_specs=vmem,
        scratch_shapes=[lhs, pltpu.SemaphoreType.DMA((2 * len(a_own),))],
        compiler_params=params,
        name="near",
    )(*a_own, *a_core, w_own, w_core)
    return pl.pallas_call(
        last_kernel,
        out_shape=jax.ShapeDtypeStruct((BLK, cols), bf16),
        in_specs=[hbm] * (2 * len(a_own) + 4) + [vmem],
        out_specs=hbm,
        scratch_shapes=[
            lhs,
            pltpu.VMEM((2, 4, 4, share, cols), bf16),
            pltpu.VMEM((BLK, cols), bf16),
            pltpu.SemaphoreType.DMA((2 * len(a_own) + 10,)),
        ],
        compiler_params=params,
        name="last",
    )(*a_z, *a_zc, *quarters, near)


def solution(mesh):
    in_specs = (
        P("ctx", "head", None),
        P("ctx", "head", None),
        P("ctx", "head", None),
        P("head", None),
        P(),
        P("ctx", "head", None),
    )
    out_specs = P("ctx", "head")
    return jax.shard_map(local, mesh=mesh, in_specs=in_specs, out_specs=out_specs, check_vma=False)
```
